32 devices in a mesh: fsdp: 32 (over z, y, x, core).
Axes of the slice: x: 2, y: 2, z: 4, core: 2. Of those that a mesh axis runs over, the one named last changes fastest.
Arguments:
- images: bfloat16 [256, 197, 768], P('fsdp'), may hold values from -6 to 6
- images_of: int32 [128], P('fsdp'), may hold values from 1 to 2
- cotangent: bfloat16 [256, 197, 768], P('fsdp'), may hold values from -6 to 6
- ln1_gain: bfloat16 [768], P('fsdp'), may hold values from 0.099609375 to 1.8984375
- ln1_shift: bfloat16 [768], P('fsdp'), may hold values from -1 to 1
- w_qkv: bfloat16 [768, 2304], P('fsdp'), may hold values from -0.21875 to 0.21875
- query_bias: bfloat16 [768], P('fsdp'), may hold values from -1 to 1
- value_bias: bfloat16 [768], P('fsdp'), may hold values from -1 to 1
- w_out: bfloat16 [768, 768], P('fsdp'), may hold values from -1.25 to 1.25
- out_bias: bfloat16 [768], P('fsdp'), may hold values from -1 to 1
- ln2_gain: bfloat16 [768], P('fsdp'), may hold values from 0.099609375 to 1.8984375
- ln2_shift: bfloat16 [768], P('fsdp'), may hold values from -1 to 1
- w_first: bfloat16 [768, 3072], P('fsdp'), may hold values from -0.21875 to 0.21875
- first_bias: bfloat16 [3072], P('fsdp'), may hold values from -1 to 1
- w_second: bfloat16 [3072, 768], P('fsdp'), may hold values from -0.109375 to 0.109375
- second_bias: bfloat16 [768], P('fsdp'), may hold values from -1 to 1
Outputs:
- output: bfloat16 [256, 197, 768], P('fsdp')
- input_grad: bfloat16 [256, 197, 768], P('fsdp')
- grad_ln1_gain: float32 [768], P('fsdp')
- grad_ln1_shift: float32 [768], P('fsdp')
- grad_w_qkv: float32 [768, 2304], P('fsdp')
- grad_query_bias: float32 [768], P('fsdp')
- grad_value_bias: float32 [768], P('fsdp')
- grad_w_out: float32 [768, 768], P('fsdp')
- grad_out_bias: float32 [768], P('fsdp')
- grad_ln2_gain: float32 [768], P('fsdp')
- grad_ln2_shift: float32 [768], P('fsdp')
- grad_w_first: float32 [768, 3072], P('fsdp')
- grad_first_bias: float32 [3072], P('fsdp')
- grad_w_second: float32 [3072, 768], P('fsdp')
- grad_second_bias: float32 [768], P('fsdp')
The draws below stay inside these ranges and needn't reach their ends.
Inputs may be any that keep to these rules, and one draw needn't show every extreme that they name: Slot 2t holds an image; slot 2t + 1 holds one only where images_of[t] is 2.
All inputs are finite; a program needn't handle non-finite values.
Results may differ from the reference program's by a relative error of at most 0.013.
Values may be sent and summed in bfloat16 or wider, within the bound.
No kernel may reach another device: no remote copies, remote signals or barrier semaphores. Data moves between devices by JAX's collectives and lax.ppermute only.
A program may use at most 256 MiB of HBM per device.

```python
import jax
import jax.numpy as jnp
from jax import lax

D = 768
FF = 3072
HEAD_DIM = 64
SEQ = 197
MICRO = 4
SLOTS = 256
TABLE = 128
N_FSDP = 32


def place_ends(array, stream_key, low, largest):
    shape = array.shape
    place = [jax.random.randint(jax.random.fold_in(stream_key, axis), (), 0, shape[axis]) for axis in range(len(shape))]
    array = array.at[tuple(place)].set(low)
    longest = shape.index(max(shape))
    place[longest] = (place[longest] + 1) % shape[longest]
    return array.at[tuple(place)].set(largest)


def raised(drawn, stream_key, source, target, blocks, factor):
    def block_of(dim):
        return (jnp.arange(drawn.shape[dim]) // (drawn.shape[dim] // blocks)).reshape((-1,) + (1,) * (drawn.ndim - 1 - dim))

    one_side = jax.random.permutation(stream_key, blocks)[block_of(target)]
    other_side = (block_of(target) + blocks // 2) % blocks
    return jnp.where((block_of(source) == one_side) | (block_of(source) == other_side), factor * drawn, drawn)


def block_scale(own_key, shape, cuts, low, largest):
    def one(dim, parts):
        draws = jax.random.uniform(jax.random.fold_in(jax.random.fold_in(own_key, 6), dim), (parts,), jnp.float32, low / len(cuts), largest / len(cuts))
        return jnp.repeat(jnp.exp(draws), shape[dim] // parts).reshape((-1,) + (1,) * (len(shape) - dim - 1))

    loudness = one(*cuts[0])
    for cut in cuts[1:]:
        loudness = loudness * one(*cut)
    return loudness


def normal_values(stream_key, extent, deviation, reach, split=(), held_as=jnp.bfloat16):
    values = jax.random.normal(stream_key, extent, jnp.float32) * deviation
    if len(split) > 0:
        values = block_scale(stream_key, extent, split, -0.22, 0.18) * values
    return jnp.clip(values, min=-reach, max=reach).astype(held_as)


def noise_with(stream_key, shape, scale, reach, pieces, heavy, held_as=jnp.bfloat16):
    entries = scale * jax.random.normal(stream_key, shape, jnp.float32)
    if pieces:
        entries = entries * block_scale(stream_key, shape, pieces, -0.22, 0.18)
    return jnp.clip(raised(entries, jax.random.fold_in(stream_key, 3), *heavy), -reach, reach).astype(held_as)


def setup_inputs(seed: int = 0) -> dict:
    key_list = jax.random.split(jax.random.key(seed), 17)
    return {
        "images": normal_values(key_list[0], (SLOTS, SEQ, D), 1.0, 6.0, ((0, 32),)),
        "images_of": place_ends(jax.random.randint(key_list[1], (TABLE,), 1, 3), jax.random.fold_in(key_list[1], 1), 1, 2).astype(jnp.int32),
        "cotangent": noise_with(key_list[2], (SLOTS, SEQ, D), 1.0, 6.0, ((0, 32),), (0, 2, 32, 2.75)),
        "ln1_gain": jnp.clip(1.0 + 0.18 * jax.random.normal(key_list[3], (D,), jnp.float32), 0.099609375, 1.8984375).astype(jnp.bfloat16),
        "ln1_shift": normal_values(key_list[4], (D,), 0.2, 1.0, ((0, 32),)),
        "w_qkv": normal_values(key_list[5], (D, 3 * D), D ** -0.5, 0.21875, ((0, 32),)),
        "query_bias": normal_values(key_list[6], (D,), 0.2, 1.0, ((0, 32),)),
        "value_bias": normal_values(key_list[7], (D,), 0.2, 1.0, ((0, 32),)),
        "w_out": normal_values(key_list[8], (D, D), (D // 32) ** -0.5, 1.25, ((0, 32),)),
        "out_bias": normal_values(key_list[9], (D,), 0.2, 1.0, ((0, 32),)),
        "ln2_gain": jnp.clip(1.0 + 0.18 * jax.random.normal(key_list[10], (D,), jnp.float32), 0.099609375, 1.8984375).astype(jnp.bfloat16),
        "ln2_shift": normal_values(key_list[11], (D,), 0.2, 1.0, ((0, 32),)),
        "w_first": normal_values(key_list[12], (D, FF), D ** -0.5, 0.21875, ((0, 32),)),
        "first_bias": normal_values(key_list[13], (FF,), 0.2, 1.0, ((0, 32),)),
        "w_second": normal_values(key_list[14], (FF, D), FF ** -0.5, 0.109375, ((0, 32),)),
        "second_bias": normal_values(key_list[15], (D,), 0.2, 1.0, ((0, 32),)),
    }


@jax.custom_vjp
def low(v):
    return lax.optimization_barrier(v.astype(jnp.bfloat16)).astype(jnp.float32)

@jax.custom_vjp
def low_back(v):
    return v

def low_keep(v):
    return (low(v), None)

def low_pass(kept, grad):
    return (grad,)

def back_keep(v):
    return (v, None)

def back_low(kept, grad):
    return (low(grad),)
low.defvjp(low_keep, low_pass)
low_back.defvjp(back_keep, back_low)
highest = lax.Precision.HIGHEST

def layer_norm(rows, gain, shift):
    average = lax.optimization_barrier(jnp.mean(rows, axis=-1, keepdims=True))
    centred = rows - average
    variance = lax.optimization_barrier(jnp.mean(centred * centred, axis=-1, keepdims=True))
    return centred * lax.rsqrt(variance + 1e-06) * gain + shift

def encode(params, slots_in, slot_live):
    ln1_gain, ln1_shift, w_qkv, query_bias, value_bias, w_out, out_bias, ln2_gain, ln2_shift, w_first, first_bias, w_second, second_bias = params
    count, length, width = slots_in.shape
    heads = width // HEAD_DIM
    normed_one = low(layer_norm(slots_in, ln1_gain, ln1_shift))
    projected = jnp.einsum('bsd,de->bse', normed_one, w_qkv, precision=highest)
    query = low(low_back(projected[..., :width] + query_bias)).reshape(count, length, heads, HEAD_DIM)
    key_rows = low(low_back(projected[..., width:2 * width])).reshape(count, length, heads, HEAD_DIM)
    value_rows = low(low_back(projected[..., 2 * width:] + value_bias)).reshape(count, length, heads, HEAD_DIM)
    scores = low_back(jnp.einsum('bqhd,bkhd->bhqk', query, key_rows, precision=highest) * HEAD_DIM ** (-0.5))
    probs = low(jax.nn.softmax(scores, axis=-1))
    mixed = jnp.einsum('bhqk,bkhd->bqhd', probs, value_rows, precision=highest).reshape(count, length, width)
    mixed = low(low_back(mixed))
    attended = jnp.einsum('bsd,de->bse', mixed, w_out, precision=highest) + out_bias
    resid = slots_in + low_back(attended)
    normed_two = low(layer_norm(resid, ln2_gain, ln2_shift))
    hidden = low_back(jnp.einsum('bsd,df->bsf', normed_two, w_first, precision=highest) + first_bias)
    active = low(jax.nn.gelu(hidden, approximate=False))
    branch = jnp.einsum('bsf,fd->bsd', active, w_second, precision=highest) + second_bias
    return (resid + low_back(branch)) * slot_live[:, None, None]

def reference(images, images_of, cotangent, ln1_gain, ln1_shift, w_qkv, query_bias, value_bias, w_out, out_bias, ln2_gain, ln2_shift, w_first, first_bias, w_second, second_bias):
    slot_index = jnp.arange(SLOTS, dtype=jnp.int32)
    live = (slot_index % 2 < jnp.repeat(images_of, 2)).astype(jnp.float32)
    params = tuple((p.astype(jnp.float32) for p in (ln1_gain, ln1_shift, w_qkv, query_bias, value_bias, w_out, out_bias, ln2_gain, ln2_shift, w_first, first_bias, w_second, second_bias)))
    live_groups = live.reshape(N_FSDP, 2 * MICRO)

    def forward(slots_in, weights):
        grouped = slots_in.reshape(N_FSDP, 2 * MICRO, SEQ, D)
        step = jax.checkpoint(lambda pair: encode(weights, pair[0], pair[1]))
        return lax.map(step, (grouped, live_groups)).reshape(SLOTS, SEQ, D)
    result, pull = jax.vjp(forward, images.astype(jnp.float32), params)
    input_grad, grads = pull(cotangent.astype(jnp.float32))
    return (result.astype(jnp.bfloat16), input_grad.astype(jnp.bfloat16), grads[0], grads[1], grads[2], grads[3], grads[4], grads[5], grads[6], grads[7], grads[8], grads[9], grads[10], grads[11], grads[12])
```

```python
import functools

import jax
import jax.numpy as jnp
from jax import lax
from jax.experimental import pallas as pl
from jax.experimental.pallas import tpu as pltpu
from jax.sharding import PartitionSpec as P

HEAD_DIM = 64
LANES = 128
ROW_TILE = 16
LOG2E = 1.4426950408889634
VMEM_BYTES = 60 * 1024 * 1024
F32 = jnp.float32
BF16 = jnp.bfloat16
GAIN1, SHIFT1, QUERY_BIAS, VALUE_BIAS, OUT_BIAS, GAIN2, SHIFT2, SECOND_BIAS = range(8)


def dot(left, right):
    return lax.dot_general(left, right, (((1,), (0,)), ((), ())), preferred_element_type=F32)


def dot_cols(left, right):
    return lax.dot_general(left, right, (((1,), (1,)), ((), ())), preferred_element_type=F32)


def dot_rows(left, right):
    return lax.dot_general(left, right, (((0,), (0,)), ((), ())), preferred_element_type=F32)


def unit_parts(rows):
    average = jnp.mean(rows, axis=-1, keepdims=True)
    centred = rows - average
    variance = jnp.mean(centred * centred, axis=-1, keepdims=True)
    inverse = lax.rsqrt(variance + 1e-06)
    return centred * inverse, inverse


def norm_back(grad_out, unit_rows, inverse, gain):
    scaled = grad_out * gain
    first = jnp.mean(scaled, axis=-1, keepdims=True)
    second = jnp.mean(scaled * unit_rows, axis=-1, keepdims=True)
    return inverse * (scaled - first - unit_rows * second)


def column_sum(values):
    return jnp.sum(values.astype(F32), axis=0, keepdims=True)


def attend_kernel(length, x_ref, table_ref, w_qkv_ref, w_out_ref, qkv_ref, mixed_ref, resid_ref, stat_ref):
    rows = x_ref[0].astype(F32)
    seq, width = rows.shape
    row = lambda index: table_ref[index : index + 1, :]
    unit_rows, _ = unit_parts(rows)
    normed = (unit_rows * row(GAIN1) + row(SHIFT1)).astype(BF16)
    projected = dot(normed, w_qkv_ref[...])
    inside = lax.broadcasted_iota(jnp.int32, (seq, 1), 0) < length
    query = jnp.where(inside, projected[:, :width] + row(QUERY_BIAS), 0.0).astype(BF16)
    keys = jnp.where(inside, projected[:, width : 2 * width], 0.0).astype(BF16)
    values = jnp.where(inside, projected[:, 2 * width :] + row(VALUE_BIAS), 0.0).astype(BF16)
    qkv_ref[0, :, :width] = query
    qkv_ref[0, :, width : 2 * width] = keys
    qkv_ref[0, :, 2 * width :] = values
    outside = jnp.where(lax.broadcasted_iota(jnp.int32, (1, seq), 1) < length, 0.0, -1e30)
    low_half = lax.broadcasted_iota(jnp.int32, (1, LANES), 1) < HEAD_DIM
    lane = lax.broadcasted_iota(jnp.int32, (1, LANES), 1)
    stats = jnp.zeros((seq, LANES), F32)
    for pair in range(width // LANES):
        columns = slice(pair * LANES, (pair + 1) * LANES)
        query_pair, key_pair, value_pair = query[:, columns], keys[:, columns], values[:, columns]
        halves = []
        for half in range(2):
            mine = low_half if half == 0 else jnp.logical_not(low_half)
            scores = dot_cols(jnp.where(mine, query_pair, 0), key_pair) * (LOG2E * HEAD_DIM**-0.5) + outside
            top = jnp.max(scores, axis=-1, keepdims=True)
            expos = jnp.exp2(scores - top)
            total = jnp.sum(expos, axis=-1, keepdims=True)
            halves.append(dot(expos.astype(BF16), value_pair) * (1.0 / total))
            stats = jnp.where(lane == 2 * pair + half, top + jnp.log2(total), stats)
        mixed_ref[0, :, columns] = jnp.where(low_half, halves[0], halves[1]).astype(BF16)
    stat_ref[0] = stats
    resid_ref[0] = rows + dot(mixed_ref[0], w_out_ref[...]) + row(OUT_BIAS)


def attend_back_kernel(length, d_attn_ref, w_out_ref, qkv_ref, mixed_ref, stat_ref, d_qkv_ref):
    seq, width = d_attn_ref.shape[1:]
    d_mixed = dot_cols(d_attn_ref[0], w_out_ref[...]).astype(BF16)
    inside = lax.broadcasted_iota(jnp.int32, (seq, 1), 0) < length
    low_half = lax.broadcasted_iota(jnp.int32, (1, LANES), 1) < HEAD_DIM
    scale = HEAD_DIM**-0.5
    products = (d_mixed.astype(F32) * mixed_ref[0].astype(F32)).astype(BF16)
    head_of = lax.broadcasted_iota(jnp.int32, (width, LANES), 0) // HEAD_DIM
    picks = (head_of == lax.broadcasted_iota(jnp.int32, (width, LANES), 1)).astype(BF16)
    inner = dot(products, picks)
    inner_flat = jnp.transpose(inner)
    stats_flat = jnp.transpose(stat_ref[0])
    for pair in range(width // LANES):
        at = pair * LANES
        query_pair = qkv_ref[0, :, at : at + LANES]
        key_pair = qkv_ref[0, :, width + at : width + at + LANES]
        value_pair = qkv_ref[0, :, 2 * width + at : 2 * width + at + LANES]
        d_mixed_pair = d_mixed[:, at : at + LANES]
        d_query, d_key, d_value = [], [], []
        for half in range(2):
            head = 2 * pair + half
            mine = low_half if half == 0 else jnp.logical_not(low_half)
            scores = dot_cols(key_pair, jnp.where(mine, query_pair, 0)) * (LOG2E * scale)
            probs = jnp.exp2(scores - stats_flat[head : head + 1, :])
            d_probs = dot_cols(value_pair, jnp.where(mine, d_mixed_pair, 0))
            d_scores = (probs * (d_probs - inner_flat[head : head + 1, :])).astype(BF16)
            d_value.append(dot(probs.astype(BF16), d_mixed_pair))
            d_key.append(dot(d_scores, query_pair))
            d_query.append(dot_rows(d_scores, key_pair))
        merge = lambda pieces: jnp.where(low_half, pieces[0], pieces[1])
        d_qkv_ref[0, :, at : at + LANES] = (merge(d_query) * scale).astype(BF16)
        d_qkv_ref[0, :, width + at : width + at + LANES] = jnp.where(inside, merge(d_key) * scale, 0.0).astype(BF16)
        d_qkv_ref[0, :, 2 * width + at : 2 * width + at + LANES] = jnp.where(inside, merge(d_value), 0.0).astype(BF16)


def feed_kernel(
    resid_ref, grad_ref, table_ref, first_bias_ref, w_first_ref, w_second_ref,
    out_ref, d_resid_ref, d_attn_ref, d_weights_ref, sums_ref, d_first_bias_ref,
    normed_ref, branch_ref, d_two_ref, active_ref, d_hidden_ref,
):
    step = pl.program_id(0)
    total_rows, width = resid_ref.shape
    block = w_first_ref.shape[1]
    tile = normed_ref.shape[0] // 4
    row = lambda index: table_ref[index : index + 1, :]

    @pl.when(step == 0)
    def _():
        unit_rows, _ = unit_parts(resid_ref[...])
        normed_ref[...] = (unit_rows * row(GAIN2) + row(SHIFT2)).astype(BF16)
        branch_ref[...] = jnp.zeros_like(branch_ref)
        d_two_ref[...] = jnp.zeros_like(d_two_ref)

    first_bias = first_bias_ref[0]
    bias_sum = jnp.zeros((1, block), F32)
    for part in range(total_rows // tile):
        here = slice(part * tile, (part + 1) * tile)
        hidden = dot(normed_ref[here, :], w_first_ref[...]) + first_bias
        bell = jnp.exp2(hidden * hidden * (-0.5 * LOG2E))
        near = 1.0 / (1.0 + (0.3275911 * 0.5**0.5) * jnp.abs(hidden))
        tail = 1.061405429 * near - 1.453152027
        tail = tail * near + 1.421413741
        tail = tail * near - 0.284496736
        tail = tail * near + 0.254829592
        tail = tail * near * bell * 0.5
        below = jnp.where(hidden >= 0.0, 1.0 - tail, tail)
        active = (hidden * below).astype(BF16)
        active_ref[here, :] = active
        branch_ref[here, :] += dot(active, w_second_ref[...])
        slope = below + hidden * bell * 0.3989422804014327
        d_hidden = dot_cols(grad_ref[here, :], w_second_ref[...]) * slope
        d_hidden = d_hidden.astype(BF16)
        d_hidden_ref[here, :] = d_hidden
        bias_sum += column_sum(d_hidden)
        d_two_ref[here, :] += dot_cols(d_hidden, w_first_ref[...])
    d_first_bias_ref[0] = bias_sum
    d_weights_ref[:, :block] = dot_rows(normed_ref[...], d_hidden_ref[...]).astype(BF16)
    d_weights_ref[:, block:] = dot_rows(active_ref[...], grad_ref[...]).astype(BF16)

    @pl.when(step == pl.num_programs(0) - 1)
    def _():
        resid = resid_ref[...]
        unit_rows, inverse = unit_parts(resid)
        out_ref[...] = (resid + branch_ref[...] + row(SECOND_BIAS)).astype(BF16)
        d_two = d_two_ref[...]
        sums_ref[0:1, :] = column_sum(d_two * unit_rows)
        sums_ref[1:2, :] = column_sum(d_two)
        sums_ref[2:3, :] = column_sum(grad_ref[...])
        d_resid = grad_ref[...].astype(F32) + norm_back(d_two, unit_rows, inverse, row(GAIN2))
        d_resid_ref[...] = d_resid
        d_attn = d_resid.astype(BF16)
        d_attn_ref[...] = d_attn
        sums_ref[3:4, :] = column_sum(d_attn)
        sums_ref[4:8, :] = jnp.zeros((4, width), F32)


def weight_grad_kernel(x_ref, table_ref, columns_ref, w_qkv_ref, d_qkv_ref, d_w_ref, sums_ref, norm_sums_ref, unit_ref):
    @pl.when(pl.program_id(0) == 0)
    def _():
        unit_rows, _ = unit_parts(x_ref[...].astype(F32))
        unit_ref[...] = unit_rows.astype(BF16)
        norm_sums_ref[...] = jnp.zeros_like(norm_sums_ref)

    d_qkv = d_qkv_ref[...]
    total = column_sum(d_qkv)
    unit_grad = dot_rows(unit_ref[...], d_qkv)
    gain, shift = columns_ref[:, GAIN1 : GAIN1 + 1], columns_ref[:, SHIFT1 : SHIFT1 + 1]
    d_w_ref[...] = (unit_grad * gain + shift * total).astype(BF16)
    sums_ref[...] = jnp.broadcast_to(total, sums_ref.shape)
    weight = w_qkv_ref[...].astype(F32)
    norm_sums_ref[:, 0:1] += jnp.sum(unit_grad * weight, axis=1, keepdims=True)
    norm_sums_ref[:, 1:2] += jnp.sum(total * weight, axis=1, keepdims=True)


def input_grad_kernel(x_ref, table_ref, d_qkv_ref, w_qkv_ref, d_resid_ref, out_ref):
    d_one = dot_cols(d_qkv_ref[...], w_qkv_ref[...])
    unit_rows, inverse = unit_parts(x_ref[...].astype(F32))
    change = norm_back(d_one, unit_rows, inverse, table_ref[GAIN1 : GAIN1 + 1, :])
    out_ref[...] = (d_resid_ref[...] + change).astype(BF16)


def params():
    return pltpu.CompilerParams(vmem_limit_bytes=VMEM_BYTES)


def cost(flops, moved, exps=0):
    return pl.CostEstimate(flops=int(flops), bytes_accessed=int(moved), transcendentals=int(exps))


def once(shape):
    zeros = (0,) * len(shape)
    return pl.BlockSpec(shape, lambda *_: zeros)


def attend(x, table, weights, length):
    count, seq, width = x.shape
    per_slot = lambda cols: pl.BlockSpec((1, seq, cols), lambda slot: (slot, 0, 0))
    rows = count * seq
    return pl.pallas_call(
        functools.partial(attend_kernel, length),
        grid=(count,),
        in_specs=[
            per_slot(width),
            once(table.shape),
            pl.BlockSpec((width, 3 * width), lambda slot: (0, 0)),
            pl.BlockSpec((width, width), lambda slot: (0, 3)),
        ],
        out_specs=[per_slot(3 * width), per_slot(width), per_slot(width), per_slot(LANES)],
        out_shape=[
            jax.ShapeDtypeStruct((count, seq, 3 * width), BF16),
            jax.ShapeDtypeStruct((count, seq, width), BF16),
            jax.ShapeDtypeStruct((count, seq, width), F32),
            jax.ShapeDtypeStruct((count, seq, LANES), F32),
        ],
        compiler_params=params(),
        cost_estimate=cost(12 * rows * width * width, rows * width * 14, rows * seq * 12),
    )(x, table, weights, weights)


def attend_back(d_attn, weights, qkv, mixed, stats, length):
    count, seq, width = d_attn.shape
    per_slot = lambda cols: pl.BlockSpec((1, seq, cols), lambda slot: (slot, 0, 0))
    rows = count * seq
    return pl.pallas_call(
        functools.partial(attend_back_kernel, length),
        grid=(count,),
        in_specs=[
            per_slot(width),
            pl.BlockSpec((width, width), lambda slot: (0, 3)),
            per_slot(3 * width),
            per_slot(width),
            per_slot(LANES),
        ],
        out_specs=per_slot(3 * width),
        out_shape=jax.ShapeDtypeStruct((count, seq, 3 * width), BF16),
        compiler_params=params(),
        cost_estimate=cost(10 * rows * width * width, rows * width * 16, rows * seq * 12),
    )(d_attn, weights, qkv, mixed, stats)


def feed(resid, grad, table, first_bias, weights):
    rows, width = resid.shape
    steps, _, block = first_bias.shape
    ff = steps * block
    column = lambda shift: pl.BlockSpec((width, block), lambda step: (0, 2 * step + shift))
    keep = lambda shape: pl.BlockSpec(shape, lambda step: (0, 0), pipeline_mode=pl.Buffered(1))
    return pl.pallas_call(
        feed_kernel,
        grid=(steps,),
        in_specs=[
            keep((rows, width)),
            keep((rows, width)),
            keep(table.shape),
            pl.BlockSpec((1, 1, block), lambda step: (step, 0, 0)),
            column(0),
            column(1),
        ],
        out_specs=[
            keep((rows, width)),
            keep((rows, width)),
            keep((rows, width)),
            pl.BlockSpec((width, 2 * block), lambda step: (0, step)),
            keep((8, width)),
            pl.BlockSpec((1, 1, block), lambda step: (step, 0, 0)),
        ],
        out_shape=[
            jax.ShapeDtypeStruct((rows, width), BF16),
            jax.ShapeDtypeStruct((rows, width), F32),
            jax.ShapeDtypeStruct((rows, width), BF16),
            jax.ShapeDtypeStruct((width, 2 * ff), BF16),
            jax.ShapeDtypeStruct((8, width), F32),
            jax.ShapeDtypeStruct((steps, 1, block), F32),
        ],
        scratch_shapes=[
            pltpu.VMEM((rows, width), BF16),
            pltpu.VMEM((rows, width), F32),
            pltpu.VMEM((rows, width), F32),
            pltpu.VMEM((rows, block), BF16),
            pltpu.VMEM((rows, block), BF16),
        ],
        compiler_params=params(),
        cost_estimate=cost(12 * rows * width * ff, rows * width * 16 + 8 * width * ff, 2 * rows * ff),
    )(resid, grad, table, first_bias, weights, weights)


def weight_grad(x, table, columns, weights, d_qkv):
    rows, width = x.shape
    wide = d_qkv.shape[1]
    block = 256
    keep = lambda shape: pl.BlockSpec(shape, lambda step: (0, 0), pipeline_mode=pl.Buffered(1))
    moving = lambda high: pl.BlockSpec((high, block), lambda step: (0, step))
    return pl.pallas_call(
        weight_grad_kernel,
        grid=(wide // block,),
        in_specs=[keep((rows, width)), keep(table.shape), keep(columns.shape), moving(width), moving(rows)],
        out_specs=[moving(width), moving(8), keep((width, LANES))],
        out_shape=[
            jax.ShapeDtypeStruct((width, wide + LANES), BF16),
            jax.ShapeDtypeStruct((8, wide), F32),
            jax.ShapeDtypeStruct((width, LANES), F32),
        ],
        scratch_shapes=[pltpu.VMEM((rows, width), BF16)],
        compiler_params=params(),
        cost_estimate=cost(2 * rows * width * wide, 2 * rows * (wide + width) + 4 * wide * width),
    )(x, table, columns, weights, d_qkv)


def input_grad(x, table, d_qkv, weights, d_resid):
    rows, width = x.shape
    wide = d_qkv.shape[1]
    tile = rows // 4
    part = lambda cols: pl.BlockSpec((tile, cols), lambda step: (step, 0))
    return pl.pallas_call(
        input_grad_kernel,
        grid=(rows // tile,),
        in_specs=[
            part(width),
            once(table.shape),
            part(wide),
            pl.BlockSpec((width, wide), lambda step: (0, 0)),
            part(width),
        ],
        out_specs=part(width),
        out_shape=jax.ShapeDtypeStruct((rows, width), BF16),
        compiler_params=params(),
        cost_estimate=cost(2 * rows * width * wide, rows * (2 * wide + 8 * width)),
    )(x, table, d_qkv, weights, d_resid)


def gather(value):
    return lax.all_gather(value, "fsdp", axis=0, tiled=True)


def scatter(value):
    return lax.psum_scatter(value, "fsdp", scatter_dimension=0, tiled=True)


def on_device(
    images,
    images_of,
    cotangent,
    ln1_gain,
    ln1_shift,
    w_qkv,
    query_bias,
    value_bias,
    w_out,
    out_bias,
    ln2_gain,
    ln2_shift,
    w_first,
    first_bias,
    w_second,
    second_bias,
):
    count, length, width = images.shape
    own = w_qkv.shape[0]
    wide = w_qkv.shape[1]
    ff = w_first.shape[1]
    chunks = ff // width
    seq = -(-length // ROW_TILE) * ROW_TILE
    rows = count * seq
    slot_index = jnp.arange(count, dtype=jnp.int32)
    slot_live = (slot_index % 2 < jnp.repeat(images_of, 2)).astype(BF16)[:, None, None]

    small = jnp.stack(
        [ln1_gain, ln1_shift, query_bias, value_bias, out_bias, ln2_gain, ln2_shift, second_bias], axis=1
    )
    small = jnp.concatenate([small, first_bias.reshape(own, chunks)], axis=1)
    small = jnp.pad(small, ((0, 0), (0, LANES - small.shape[1])))
    first_parts = w_first.reshape(own, width, chunks).transpose(0, 2, 1)
    feed_shard = jnp.stack([first_parts, w_second.reshape(own, chunks, width)], axis=2)
    attn_weights = gather(jnp.concatenate([w_qkv, w_out, small], axis=1))
    feed_weights = gather(feed_shard.reshape(own, 2 * ff))
    columns = attn_weights[:, wide + width :].astype(F32)
    table = columns[:, :16].T
    bias_rows = table[8 : 8 + chunks].reshape(chunks, 1, width)

    pad = ((0, 0), (0, seq - length), (0, 0))
    x = jnp.pad(images, pad)
    grad = jnp.pad(cotangent * slot_live, pad).reshape(rows, width)

    qkv, mixed, resid, stats = attend(x, table, attn_weights, length)
    out, d_resid, d_attn, d_feed, feed_sums, d_first_bias = feed(
        resid.reshape(rows, width), grad, table, bias_rows, feed_weights
    )
    d_w_out = dot_rows(mixed.reshape(rows, width), d_attn).astype(BF16)
    d_feed = scatter(jnp.concatenate([d_feed, d_w_out], axis=1))
    d_qkv = attend_back(d_attn.reshape(count, seq, width), attn_weights, qkv, mixed, stats, length)
    d_qkv = d_qkv.reshape(rows, wide)
    x_rows = x.reshape(rows, width)
    d_w_qkv, qkv_sums, norm_sums = weight_grad(x_rows, table, columns, attn_weights, d_qkv)
    ends = jnp.concatenate(
        [
            norm_sums[:, :2],
            qkv_sums[0, :width][:, None],
            qkv_sums[0, 2 * width :][:, None],
            feed_sums[:4].T,
            d_first_bias.reshape(chunks, width).T,
        ],
        axis=1,
    )
    ends = jnp.pad(ends, ((0, 0), (0, LANES - ends.shape[1]))).astype(BF16)
    d_qkv_all = scatter(lax.dynamic_update_slice(d_w_qkv, ends, (0, wide)))
    d_x = input_grad(x_rows, table, d_qkv, attn_weights, d_resid)

    output = out.reshape(count, seq, width)[:, :length] * slot_live
    d_x = d_x.reshape(count, seq, width)[:, :length]
    d_w_out = d_feed[:, 2 * ff :].astype(F32)
    d_feed = d_feed[:, : 2 * ff].astype(F32).reshape(own, chunks, 2, width)
    d_w_first = d_feed[:, :, 0].transpose(0, 2, 1).reshape(own, ff)
    d_w_second = d_feed[:, :, 1].reshape(own * chunks, width)
    d_w_qkv = d_qkv_all[:, :wide].astype(F32)
    ends = d_qkv_all[:, wide:].astype(F32)
    return (
        output,
        d_x,
        ends[:, 0],
        ends[:, 1],
        d_w_qkv,
        ends[:, 2],
        ends[:, 3],
        d_w_out,
        ends[:, 7],
        ends[:, 4],
        ends[:, 5],
        d_w_first,
        ends[:, 8 : 8 + chunks].reshape(own * chunks),
        d_w_second,
        ends[:, 6],
    )


def solution(mesh):
    flat, rows = P("fsdp"), P("fsdp", None)
    slots = P("fsdp", None, None)
    placed = (slots, flat, slots, flat, flat, rows, flat, flat, rows, flat, flat, flat, rows, flat, rows, flat)
    outs = (slots, slots, flat, flat, rows, flat, flat, rows, flat, flat, flat, rows, flat, rows, flat)
    return jax.shard_map(on_device, mesh=mesh, in_specs=placed, out_specs=outs, check_vma=False)
```

```python
import functools

import jax
import jax.numpy as jnp
from jax import lax
from jax.experimental import pallas as pl
from jax.experimental.pallas import tpu as pltpu
from jax.sharding import PartitionSpec as P

HEAD_DIM = 64
LANES = 128
ROW_TILE = 16
LOG2E = 1.4426950408889634
VMEM_BYTES = 60 * 1024 * 1024
F32 = jnp.float32
BF16 = jnp.bfloat16
GAIN1, SHIFT1, QUERY_BIAS, VALUE_BIAS, OUT_BIAS, GAIN2, SHIFT2, SECOND_BIAS = range(8)


def dot(left, right):
    return lax.dot_general(left, right, (((1,), (0,)), ((), ())), preferred_element_type=F32)


def dot_cols(left, right):
    return lax.dot_general(left, right, (((1,), (1,)), ((), ())), preferred_element_type=F32)


def dot_rows(left, right):
    return lax.dot_general(left, right, (((0,), (0,)), ((), ())), preferred_element_type=F32)


def unit_parts(rows):
    average = jnp.mean(rows, axis=-1, keepdims=True)
    centred = rows - average
    variance = jnp.mean(centred * centred, axis=-1, keepdims=True)
    inverse = lax.rsqrt(variance + 1e-06)
    return centred * inverse, inverse


def norm_back(grad_out, unit_rows, inverse, gain):
    scaled = grad_out * gain
    first = jnp.mean(scaled, axis=-1, keepdims=True)
    second = jnp.mean(scaled * unit_rows, axis=-1, keepdims=True)
    return inverse * (scaled - first - unit_rows * second)


def column_sum(values):
    return jnp.sum(values.astype(F32), axis=0, keepdims=True)


def attend_kernel(length, x_ref, table_ref, w_qkv_ref, w_out_ref, qkv_ref, mixed_ref, resid_ref, stat_ref):
    rows = x_ref[0].astype(F32)
    seq, width = rows.shape
    row = lambda index: table_ref[index : index + 1, :]
    unit_rows, _ = unit_parts(rows)
    normed = (unit_rows * row(GAIN1) + row(SHIFT1)).astype(BF16)
    projected = dot(normed, w_qkv_ref[...])
    inside = lax.broadcasted_iota(jnp.int32, (seq, 1), 0) < length
    query = jnp.where(inside, projected[:, :width] + row(QUERY_BIAS), 0.0).astype(BF16)
    keys = jnp.where(inside, projected[:, width : 2 * width], 0.0).astype(BF16)
    values = jnp.where(inside, projected[:, 2 * width :] + row(VALUE_BIAS), 0.0).astype(BF16)
    qkv_ref[0, :, :width] = query
    qkv_ref[0, :, width : 2 * width] = keys
    qkv_ref[0, :, 2 * width :] = values
    outside = jnp.where(lax.broadcasted_iota(jnp.int32, (1, seq), 1) < length, 0.0, -1e30)
    low_half = lax.broadcasted_iota(jnp.int32, (1, LANES), 1) < HEAD_DIM
    lane = lax.broadcasted_iota(jnp.int32, (1, LANES), 1)
    stats = jnp.zeros((seq, LANES), F32)
    for pair in range(width // LANES):
        columns = slice(pair * LANES, (pair + 1) * LANES)
        query_pair, key_pair, value_pair = query[:, columns], keys[:, columns], values[:, columns]
        halves = []
        for half in range(2):
            mine = low_half if half == 0 else jnp.logical_not(low_half)
            scores = dot_cols(jnp.where(mine, query_pair, 0), key_pair) * (LOG2E * HEAD_DIM**-0.5) + outside
            top = jnp.max(scores, axis=-1, keepdims=True)
            expos = jnp.exp2(scores - top)
            total = jnp.sum(expos, axis=-1, keepdims=True)
            halves.append(dot(expos.astype(BF16), value_pair) * (1.0 / total))
            stats = jnp.where(lane == 2 * pair + half, top + jnp.log2(total), stats)
        mixed_ref[0, :, columns] = jnp.where(low_half, halves[0], halves[1]).astype(BF16)
    stat_ref[0] = stats
    resid_ref[0] = rows + dot(mixed_ref[0], w_out_ref[...]) + row(OUT_BIAS)


def attend_back_kernel(length, d_attn_ref, w_out_ref, qkv_ref, mixed_ref, stat_ref, d_qkv_ref):
    seq, width = d_attn_ref.shape[1:]
    d_mixed = dot_cols(d_attn_ref[0], w_out_ref[...]).astype(BF16)
    inside = lax.broadcasted_iota(jnp.int32, (seq, 1), 0) < length
    low_half = lax.broadcasted_iota(jnp.int32, (1, LANES), 1) < HEAD_DIM
    scale = HEAD_DIM**-0.5
    products = (d_mixed.astype(F32) * mixed_ref[0].astype(F32)).astype(BF16)
    head_of = lax.broadcasted_iota(jnp.int32, (width, LANES), 0) // HEAD_DIM
    picks = (head_of == lax.broadcasted_iota(jnp.int32, (width, LANES), 1)).astype(BF16)
    inner = dot(products, picks)
    inner_flat = jnp.transpose(inner)
    stats_flat = jnp.transpose(stat_ref[0])
    for pair in range(width // LANES):
        at = pair * LANES
        query_pair = qkv_ref[0, :, at : at + LANES]
        key_pair = qkv_ref[0, :, width + at : width + at + LANES]
        value_pair = qkv_ref[0, :, 2 * width + at : 2 * width + at + LANES]
        d_mixed_pair = d_mixed[:, at : at + LANES]
        d_query, d_key, d_value = [], [], []
        for half in range(2):
            head = 2 * pair + half
            mine = low_half if half == 0 else jnp.logical_not(low_half)
            scores = dot_cols(key_pair, jnp.where(mine, query_pair, 0)) * (LOG2E * scale)
            probs = jnp.exp2(scores - stats_flat[head : head + 1, :])
            d_probs = dot_cols(value_pair, jnp.where(mine, d_mixed_pair, 0))
            d_scores = (probs * (d_probs - inner_flat[head : head + 1, :])).astype(BF16)
            d_value.append(dot(probs.astype(BF16), d_mixed_pair))
            d_key.append(dot(d_scores, query_pair))
            d_query.append(dot_rows(d_scores, key_pair))
        merge = lambda pieces: jnp.where(low_half, pieces[0], pieces[1])
        d_qkv_ref[0, :, at : at + LANES] = (merge(d_query) * scale).astype(BF16)
        d_qkv_ref[0, :, width + at : width + at + LANES] = jnp.where(inside, merge(d_key) * scale, 0.0).astype(BF16)
        d_qkv_ref[0, :, 2 * width + at : 2 * width + at + LANES] = jnp.where(inside, merge(d_value), 0.0).astype(BF16)


def feed_kernel(
    resid_ref, grad_ref, table_ref, first_bias_ref, w_first_ref, w_second_ref,
    out_ref, d_resid_ref, d_attn_ref, d_first_ref, d_second_ref, sums_ref, d_first_bias_ref,
    normed_ref, branch_ref, d_two_ref, active_ref, d_hidden_ref,
):
    step = pl.program_id(0)
    total_rows, width = resid_ref.shape
    block = w_first_ref.shape[1]
    tile = normed_ref.shape[0] // 4
    row = lambda index: table_ref[index : index + 1, :]

    @pl.when(step == 0)
    def _():
        unit_rows, _ = unit_parts(resid_ref[...])
        normed_ref[...] = (unit_rows * row(GAIN2) + row(SHIFT2)).astype(BF16)
        branch_ref[...] = jnp.zeros_like(branch_ref)
        d_two_ref[...] = jnp.zeros_like(d_two_ref)

    first_bias = first_bias_ref[0]
    bias_sum = jnp.zeros((1, block), F32)
    for part in range(total_rows // tile):
        here = slice(part * tile, (part + 1) * tile)
        hidden = dot(normed_ref[here, :], w_first_ref[...]) + first_bias
        bell = jnp.exp2(hidden * hidden * (-0.5 * LOG2E))
        near = 1.0 / (1.0 + (0.3275911 * 0.5**0.5) * jnp.abs(hidden))
        tail = 1.061405429 * near - 1.453152027
        tail = tail * near + 1.421413741
        tail = tail * near - 0.284496736
        tail = tail * near + 0.254829592
        tail = tail * near * bell * 0.5
        below = jnp.where(hidden >= 0.0, 1.0 - tail, tail)
        active = (hidden * below).astype(BF16)
        active_ref[here, :] = active
        branch_ref[here, :] += dot(active, w_second_ref[...])
        slope = below + hidden * bell * 0.3989422804014327
        d_hidden = dot_cols(grad_ref[here, :], w_second_ref[...]) * slope
        d_hidden = d_hidden.astype(BF16)
        d_hidden_ref[here, :] = d_hidden
        bias_sum += column_sum(d_hidden)
        d_two_ref[here, :] += dot_cols(d_hidden, w_first_ref[...])
    d_first_bias_ref[0] = bias_sum
    d_first_ref[...] = dot_rows(normed_ref[...], d_hidden_ref[...]).astype(BF16)
    d_second_ref[...] = dot_rows(active_ref[...], grad_ref[...]).astype(BF16)

    @pl.when(step == pl.num_programs(0) - 1)
    def _():
        resid = resid_ref[...]
        unit_rows, inverse = unit_parts(resid)
        out_ref[...] = (resid + branch_ref[...] + row(SECOND_BIAS)).astype(BF16)
        d_two = d_two_ref[...]
        sums_ref[0:1, :] = column_sum(d_two * unit_rows)
        sums_ref[1:2, :] = column_sum(d_two)
        sums_ref[2:3, :] = column_sum(grad_ref[...])
        d_resid = grad_ref[...].astype(F32) + norm_back(d_two, unit_rows, inverse, row(GAIN2))
        d_resid_ref[...] = d_resid
        d_attn = d_resid.astype(BF16)
        d_attn_ref[...] = d_attn
        sums_ref[3:4, :] = column_sum(d_attn)
        sums_ref[4:8, :] = jnp.zeros((4, width), F32)


def weight_grad_kernel(x_ref, table_ref, columns_ref, w_qkv_ref, d_qkv_ref, d_w_ref, sums_ref, norm_sums_ref, unit_ref):
    @pl.when(pl.program_id(0) == 0)
    def _():
        unit_rows, _ = unit_parts(x_ref[...].astype(F32))
        unit_ref[...] = unit_rows.astype(BF16)
        norm_sums_ref[...] = jnp.zeros_like(norm_sums_ref)

    d_qkv = d_qkv_ref[...]
    total = column_sum(d_qkv)
    unit_grad = dot_rows(unit_ref[...], d_qkv)
    gain, shift = columns_ref[:, GAIN1 : GAIN1 + 1], columns_ref[:, SHIFT1 : SHIFT1 + 1]
    d_w_ref[...] = (unit_grad * gain + shift * total).astype(BF16)
    sums_ref[...] = jnp.broadcast_to(total, sums_ref.shape)
    weight = w_qkv_ref[...].astype(F32)
    norm_sums_ref[:, 0:1] += jnp.sum(unit_grad * weight, axis=1, keepdims=True)
    norm_sums_ref[:, 1:2] += jnp.sum(total * weight, axis=1, keepdims=True)


def input_grad_kernel(x_ref, table_ref, d_qkv_ref, w_qkv_ref, d_resid_ref, out_ref):
    d_one = dot_cols(d_qkv_ref[...], w_qkv_ref[...])
    unit_rows, inverse = unit_parts(x_ref[...].astype(F32))
    change = norm_back(d_one, unit_rows, inverse, table_ref[GAIN1 : GAIN1 + 1, :])
    out_ref[...] = (d_resid_ref[...] + change).astype(BF16)


def params():
    return pltpu.CompilerParams(vmem_limit_bytes=VMEM_BYTES)


def cost(flops, moved, exps=0):
    return pl.CostEstimate(flops=int(flops), bytes_accessed=int(moved), transcendentals=int(exps))


def once(shape):
    zeros = (0,) * len(shape)
    return pl.BlockSpec(shape, lambda *_: zeros)


def attend(x, table, weights, length):
    count, seq, width = x.shape
    per_slot = lambda cols: pl.BlockSpec((1, seq, cols), lambda slot: (slot, 0, 0))
    rows = count * seq
    return pl.pallas_call(
        functools.partial(attend_kernel, length),
        grid=(count,),
        in_specs=[
            per_slot(width),
            once(table.shape),
            pl.BlockSpec((width, 3 * width), lambda slot: (0, 0)),
            pl.BlockSpec((width, width), lambda slot: (0, 3)),
        ],
        out_specs=[per_slot(3 * width), per_slot(width), per_slot(width), per_slot(LANES)],
        out_shape=[
            jax.ShapeDtypeStruct((count, seq, 3 * width), BF16),
            jax.ShapeDtypeStruct((count, seq, width), BF16),
            jax.ShapeDtypeStruct((count, seq, width), F32),
            jax.ShapeDtypeStruct((count, seq, LANES), F32),
        ],
        compiler_params=params(),
        cost_estimate=cost(12 * rows * width * width, rows * width * 14, rows * seq * 12),
    )(x, table, weights, weights)


def attend_back(d_attn, weights, qkv, mixed, stats, length, first, slots, written):
    count, seq, width = d_attn.shape
    per_slot = lambda cols: pl.BlockSpec((1, seq, cols), lambda slot: (first + slot, 0, 0))
    rows = slots * seq
    whole = [] if written is None else [written]
    kernel = functools.partial(attend_back_kernel, length)
    return pl.pallas_call(
        kernel if written is None else lambda *refs: kernel(*refs[:5], refs[6]),
        grid=(slots,),
        in_specs=[
            per_slot(width),
            pl.BlockSpec((width, width), lambda slot: (0, 3)),
            per_slot(3 * width),
            per_slot(width),
            per_slot(LANES),
        ]
        + [pl.BlockSpec(memory_space=pl.ANY)] * len(whole),
        out_specs=per_slot(3 * width),
        out_shape=jax.ShapeDtypeStruct((count, seq, 3 * width), BF16),
        input_output_aliases={5: 0} if whole else {},
        compiler_params=params(),
        cost_estimate=cost(10 * rows * width * width, rows * width * 16, rows * seq * 12),
    )(d_attn, weights, qkv, mixed, stats, *whole)


def feed(resid, grad, table, first_bias, weights):
    rows, width = resid.shape
    steps, _, block = first_bias.shape
    ff = steps * block
    column = lambda shift: pl.BlockSpec((width, block), lambda step: (0, 2 * step + shift))
    keep = lambda shape: pl.BlockSpec(shape, lambda step: (0, 0), pipeline_mode=pl.Buffered(1))
    return pl.pallas_call(
        feed_kernel,
        grid=(steps,),
        in_specs=[
            keep((rows, width)),
            keep((rows, width)),
            keep(table.shape),
            pl.BlockSpec((1, 1, block), lambda step: (step, 0, 0)),
            column(0),
            column(1),
        ],
        out_specs=[
            keep((rows, width)),
            keep((rows, width)),
            keep((rows, width)),
            pl.BlockSpec((width, block), lambda step: (0, step)),
            pl.BlockSpec((width, block), lambda step: (0, step)),
            keep((8, width)),
            pl.BlockSpec((1, 1, block), lambda step: (step, 0, 0)),
        ],
        out_shape=[
            jax.ShapeDtypeStruct((rows, width), BF16),
            jax.ShapeDtypeStruct((rows, width), F32),
            jax.ShapeDtypeStruct((rows, width), BF16),
            jax.ShapeDtypeStruct((width, ff), BF16),
            jax.ShapeDtypeStruct((width, ff), BF16),
            jax.ShapeDtypeStruct((8, width), F32),
            jax.ShapeDtypeStruct((steps, 1, block), F32),
        ],
        scratch_shapes=[
            pltpu.VMEM((rows, width), BF16),
            pltpu.VMEM((rows, width), F32),
            pltpu.VMEM((rows, width), F32),
            pltpu.VMEM((rows, block), BF16),
            pltpu.VMEM((rows, block), BF16),
        ],
        compiler_params=params(),
        cost_estimate=cost(12 * rows * width * ff, rows * width * 16 + 8 * width * ff, 2 * rows * ff),
    )(resid, grad, table, first_bias, weights, weights)


def weight_grad(x, table, columns, weights, d_qkv):
    rows, width = x.shape
    wide = d_qkv.shape[1]
    block = 256
    keep = lambda shape: pl.BlockSpec(shape, lambda step: (0, 0), pipeline_mode=pl.Buffered(1))
    moving = lambda high: pl.BlockSpec((high, block), lambda step: (0, step))
    return pl.pallas_call(
        weight_grad_kernel,
        grid=(wide // block,),
        in_specs=[keep((rows, width)), keep(table.shape), keep(columns.shape), moving(width), moving(rows)],
        out_specs=[moving(width), moving(8), keep((width, LANES))],
        out_shape=[
            jax.ShapeDtypeStruct((width, wide + LANES), BF16),
            jax.ShapeDtypeStruct((8, wide), F32),
            jax.ShapeDtypeStruct((width, LANES), F32),
        ],
        scratch_shapes=[pltpu.VMEM((rows, width), BF16)],
        compiler_params=params(),
        cost_estimate=cost(2 * rows * width * wide, 2 * rows * (wide + width) + 4 * wide * width),
    )(x, table, columns, weights, d_qkv)


def input_grad(x, table, d_qkv, weights, d_resid):
    rows, width = x.shape
    wide = d_qkv.shape[1]
    tile = rows // 4
    part = lambda cols: pl.BlockSpec((tile, cols), lambda step: (step, 0))
    return pl.pallas_call(
        input_grad_kernel,
        grid=(rows // tile,),
        in_specs=[
            part(width),
            once(table.shape),
            part(wide),
            pl.BlockSpec((width, wide), lambda step: (0, 0)),
            part(width),
        ],
        out_specs=part(width),
        out_shape=jax.ShapeDtypeStruct((rows, width), BF16),
        compiler_params=params(),
        cost_estimate=cost(2 * rows * width * wide, rows * (2 * wide + 8 * width)),
    )(x, table, d_qkv, weights, d_resid)


def gather(value):
    return lax.all_gather(value, "fsdp", axis=0, tiled=True)


def scatter(value):
    return lax.psum_scatter(value, "fsdp", scatter_dimension=0, tiled=True)


def swap(value, bit, devices):
    return lax.ppermute(value, "fsdp", [(i, i ^ bit) for i in range(devices)])


def my_bit(bit):
    return (lax.axis_index("fsdp") // bit) % 2


def bit_orders(devices):
    bits = [1 << k for k in range(1, devices.bit_length() - 1)]
    near, far = bits[:3], bits[3:]
    return [near[k:] + near[:k] + far for k in range(3)]


def pair_up(mine, other, axis, bit):
    shape = mine.shape[:axis] + (2,) + mine.shape[axis:]
    is_mine = lax.broadcasted_iota(jnp.int32, shape, axis) == my_bit(bit)
    return jnp.where(is_mine, jnp.expand_dims(mine, axis), jnp.expand_dims(other, axis))


def pair_gather(shard, devices):
    own = shard.shape[0]
    third = own // 3
    parts = []
    for k, order in enumerate(bit_orders(devices)):
        part, held = shard[k * third : (k + 1) * third], []
        for bit in reversed(order):
            other = swap(part, bit, devices)
            axis = sum(one > bit for one in held)
            held.append(bit)
            part = pair_up(part, other, axis, bit)
        parts.append(part.reshape(devices // 2, third, -1))
    mine = jnp.concatenate(parts, axis=1)
    whole = pair_up(mine, swap(mine, 1, devices), 1, 1)
    return whole.reshape(devices * own, -1)


def halve(value, axis, bit):
    mine = my_bit(bit)
    pick = lambda which: lax.dynamic_index_in_dim(value, which, axis, keepdims=False)
    return pick(1 - mine), pick(mine)


def add(left, right):
    return left.astype(F32) + right.astype(F32)


class PairScatter:
    def __init__(self, arrays, devices):
        self.devices = devices
        halves = [halve(one.reshape(devices // 2, 2, -1, one.shape[1]), 1, 1) for one in arrays]
        join = lambda pieces: pieces[0] if len(pieces) == 1 else jnp.concatenate(pieces, axis=-1)
        self.keep = [join([half[1] for half in halves])]
        self.coming = [swap(join([half[0] for half in halves]), 1, devices)]
        self.level = 0
        self.orders = bit_orders(devices)
        self.bits = sorted(self.orders[0], reverse=True)

    def step(self, token=None):
        sums = [add(one, two).astype(BF16) for one, two in zip(self.keep, self.coming, strict=True)]
        if self.level == 0:
            own = sums[0].shape[1]
            third = own // 3
            shape = (2,) * len(self.bits) + (third, -1)
            sums = [sums[0][:, k * third : (k + 1) * third].reshape(shape) for k in range(3)]
            self.left = [list(self.bits) for _ in range(3)]
        self.keep, sends = [], []
        for k, value in enumerate(sums):
            bit = self.orders[k][self.level]
            axis = self.left[k].index(bit)
            self.left[k].remove(bit)
            send, keep = halve(value, axis, bit)
            self.keep.append(keep)
            sends.append(send)
        if token is not None:
            *sends, token = lax.optimization_barrier((*sends, token))
        order = [one[self.level] for one in self.orders]
        self.coming = [swap(send, bit, self.devices) for send, bit in zip(sends, order, strict=True)]
        self.level += 1
        return token

    def result(self):
        while self.level < len(self.bits):
            self.step()
        return jnp.concatenate([add(one, two) for one, two in zip(self.keep, self.coming, strict=True)], axis=0)


def on_device(
    images,
    images_of,
    cotangent,
    ln1_gain,
    ln1_shift,
    w_qkv,
    query_bias,
    value_bias,
    w_out,
    out_bias,
    ln2_gain,
    ln2_shift,
    w_first,
    first_bias,
    w_second,
    second_bias,
):
    devices = lax.axis_size("fsdp")
    count, length, width = images.shape
    own = w_qkv.shape[0]
    wide = w_qkv.shape[1]
    ff = w_first.shape[1]
    chunks = ff // width
    seq = -(-length // ROW_TILE) * ROW_TILE
    rows = count * seq
    slot_index = jnp.arange(count, dtype=jnp.int32)
    slot_live = (slot_index % 2 < jnp.repeat(images_of, 2)).astype(BF16)[:, None, None]

    small = jnp.stack(
        [ln1_gain, ln1_shift, query_bias, value_bias, out_bias, ln2_gain, ln2_shift, second_bias], axis=1
    )
    small = jnp.concatenate([small, first_bias.reshape(own, chunks)], axis=1)
    small = jnp.pad(small, ((0, 0), (0, LANES - small.shape[1])))
    first_parts = w_first.reshape(own, width, chunks).transpose(0, 2, 1)
    feed_shard = jnp.stack([first_parts, w_second.reshape(own, chunks, width)], axis=2)
    attn_weights = pair_gather(jnp.concatenate([w_qkv, w_out, small], axis=1), devices)
    feed_weights = gather(feed_shard.reshape(own, 2 * ff))
    columns = attn_weights[:, wide + width :].astype(F32)
    table = columns[:, :16].T
    bias_rows = table[8 : 8 + chunks].reshape(chunks, 1, width)

    pad = ((0, 0), (0, seq - length), (0, 0))
    x = jnp.pad(images, pad)
    grad = jnp.pad(cotangent * slot_live, pad).reshape(rows, width)

    qkv, mixed, resid, stats = attend(x, table, attn_weights, length)
    out, d_resid, d_attn, d_first, d_second, feed_sums, d_first_bias = feed(
        resid.reshape(rows, width), grad, table, bias_rows, feed_weights
    )
    d_second = scatter(d_second)
    d_w_out = dot_rows(mixed.reshape(rows, width), d_attn).astype(BF16)
    feed_scatter = PairScatter([d_first, d_w_out], devices)
    d_qkv = None
    per_call = max(count // 4, 1)
    for first in range(0, count, per_call):
        if first > 0:
            d_qkv = feed_scatter.step(d_qkv)
        d_qkv = attend_back(
            d_attn.reshape(count, seq, width), attn_weights, qkv, mixed, stats, length, first, per_call, d_qkv
        )
    d_qkv = d_qkv.reshape(rows, wide)
    d_qkv = feed_scatter.step(d_qkv)
    x_rows = x.reshape(rows, width)
    d_w_qkv, qkv_sums, norm_sums = weight_grad(x_rows, table, columns, attn_weights, d_qkv)
    ends = jnp.concatenate(
        [
            norm_sums[:, :2],
            qkv_sums[0, :width][:, None],
            qkv_sums[0, 2 * width :][:, None],
            feed_sums[:4].T,
            d_first_bias.reshape(chunks, width).T,
        ],
        axis=1,
    )
    ends = jnp.pad(ends, ((0, 0), (0, LANES - ends.shape[1]))).astype(BF16)
    qkv_scatter = PairScatter([lax.dynamic_update_slice(d_w_qkv, ends, (0, wide))], devices)
    d_feed = feed_scatter.result()
    d_x = input_grad(x_rows, table, d_qkv, attn_weights, d_resid)
    d_qkv_all = qkv_scatter.result()
    d_second, d_qkv_all = lax.optimization_barrier((d_second, d_qkv_all))

    output = out.reshape(count, seq, width)[:, :length] * slot_live
    d_x = d_x.reshape(count, seq, width)[:, :length]
    d_w_out = d_feed[:, ff:]
    d_w_first = d_feed[:, :ff].reshape(own, chunks, width).transpose(0, 2, 1).reshape(own, ff)
    d_w_second = d_second.astype(F32).reshape(own * chunks, width)
    d_w_qkv = d_qkv_all[:, :wide]
    ends = d_qkv_all[:, wide:]
    return (
        output,
        d_x,
        ends[:, 0],
        ends[:, 1],
        d_w_qkv,
        ends[:, 2],
        ends[:, 3],
        d_w_out,
        ends[:, 7],
        ends[:, 4],
        ends[:, 5],
        d_w_first,
        ends[:, 8 : 8 + chunks].reshape(own * chunks),
        d_w_second,
        ends[:, 6],
    )


def solution(mesh):
    flat, rows = P("fsdp"), P("fsdp", None)
    slots = P("fsdp", None, None)
    placed = (slots, flat, slots, flat, flat, rows, flat, flat, rows, flat, flat, flat, rows, flat, rows, flat)
    outs = (slots, slots, flat, flat, rows, flat, flat, rows, flat, flat, flat, rows, flat, rows, flat)
    return jax.shard_map(on_device, mesh=mesh, in_specs=placed, out_specs=outs, check_vma=False)
```

```python
import functools

import jax
import jax.numpy as jnp
from jax import lax
from jax.experimental import pallas as pl
from jax.experimental.pallas import tpu as pltpu
from jax.sharding import PartitionSpec as P

HEAD_DIM = 64
LANES = 128
ROW_TILE = 16
LOG2E = 1.4426950408889634
VMEM_BYTES = 60 * 1024 * 1024
F32 = jnp.float32
BF16 = jnp.bfloat16
GAIN1, SHIFT1, QUERY_BIAS, VALUE_BIAS, OUT_BIAS, GAIN2, SHIFT2, SECOND_BIAS = range(8)


def dot(left, right):
    return lax.dot_general(left, right, (((1,), (0,)), ((), ())), preferred_element_type=F32)


def dot_cols(left, right):
    return lax.dot_general(left, right, (((1,), (1,)), ((), ())), preferred_element_type=F32)


def dot_rows(left, right):
    return lax.dot_general(left, right, (((0,), (0,)), ((), ())), preferred_element_type=F32)


def unit_parts(rows):
    average = jnp.mean(rows, axis=-1, keepdims=True)
    centred = rows - average
    variance = jnp.mean(centred * centred, axis=-1, keepdims=True)
    inverse = lax.rsqrt(variance + 1e-06)
    return centred * inverse, inverse


def norm_back(grad_out, unit_rows, inverse, gain):
    scaled = grad_out * gain
    first = jnp.mean(scaled, axis=-1, keepdims=True)
    second = jnp.mean(scaled * unit_rows, axis=-1, keepdims=True)
    return inverse * (scaled - first - unit_rows * second)


def column_sum(values):
    return jnp.sum(values.astype(F32), axis=0, keepdims=True)


def attend_kernel(length, x_ref, table_ref, w_qkv_ref, w_out_ref, qkv_ref, mixed_ref, resid_ref, stat_ref):
    rows = x_ref[0].astype(F32)
    seq, width = rows.shape
    row = lambda index: table_ref[index : index + 1, :]
    unit_rows, _ = unit_parts(rows)
    normed = (unit_rows * row(GAIN1) + row(SHIFT1)).astype(BF16)
    projected = dot(normed, w_qkv_ref[...])
    inside = lax.broadcasted_iota(jnp.int32, (seq, 1), 0) < length
    query = jnp.where(inside, projected[:, :width] + row(QUERY_BIAS), 0.0).astype(BF16)
    keys = jnp.where(inside, projected[:, width : 2 * width], 0.0).astype(BF16)
    values = jnp.where(inside, projected[:, 2 * width :] + row(VALUE_BIAS), 0.0).astype(BF16)
    qkv_ref[0, :, :width] = query
    qkv_ref[0, :, width : 2 * width] = keys
    qkv_ref[0, :, 2 * width :] = values
    outside = jnp.where(lax.broadcasted_iota(jnp.int32, (1, seq), 1) < length, 0.0, -1e30)
    low_half = lax.broadcasted_iota(jnp.int32, (1, LANES), 1) < HEAD_DIM
    lane = lax.broadcasted_iota(jnp.int32, (1, LANES), 1)
    stats = jnp.zeros((seq, LANES), F32)
    for pair in range(width // LANES):
        columns = slice(pair * LANES, (pair + 1) * LANES)
        query_pair, key_pair, value_pair = query[:, columns], keys[:, columns], values[:, columns]
        halves = []
        for half in range(2):
            mine = low_half if half == 0 else jnp.logical_not(low_half)
            scores = dot_cols(jnp.where(mine, query_pair, 0), key_pair) * (LOG2E * HEAD_DIM**-0.5) + outside
            top = jnp.max(scores, axis=-1, keepdims=True)
            expos = jnp.exp2(scores - top)
            total = jnp.sum(expos, axis=-1, keepdims=True)
            halves.append(dot(expos.astype(BF16), value_pair) * (1.0 / total))
            stats = jnp.where(lane == 2 * pair + half, top + jnp.log2(total), stats)
        mixed_ref[0, :, columns] = jnp.where(low_half, halves[0], halves[1]).astype(BF16)
    stat_ref[0] = stats
    resid_ref[0] = rows + dot(mixed_ref[0], w_out_ref[...]) + row(OUT_BIAS)


def attend_back_kernel(length, d_attn_ref, w_out_ref, qkv_ref, mixed_ref, stat_ref, d_qkv_ref):
    seq, width = d_attn_ref.shape[1:]
    d_mixed = dot_cols(d_attn_ref[0], w_out_ref[...]).astype(BF16)
    inside = lax.broadcasted_iota(jnp.int32, (seq, 1), 0) < length
    low_half = lax.broadcasted_iota(jnp.int32, (1, LANES), 1) < HEAD_DIM
    scale = HEAD_DIM**-0.5
    products = (d_mixed.astype(F32) * mixed_ref[0].astype(F32)).astype(BF16)
    head_of = lax.broadcasted_iota(jnp.int32, (width, LANES), 0) // HEAD_DIM
    picks = (head_of == lax.broadcasted_iota(jnp.int32, (width, LANES), 1)).astype(BF16)
    inner = dot(products, picks)
    inner_flat = jnp.transpose(inner)
    stats_flat = jnp.transpose(stat_ref[0])
    for pair in range(width // LANES):
        at = pair * LANES
        query_pair = qkv_ref[0, :, at : at + LANES]
        key_pair = qkv_ref[0, :, width + at : width + at + LANES]
        value_pair = qkv_ref[0, :, 2 * width + at : 2 * width + at + LANES]
        d_mixed_pair = d_mixed[:, at : at + LANES]
        key_flat = jnp.transpose(key_pair)
        masks = (low_half, jnp.logical_not(low_half))
        scores = [dot_cols(key_pair, jnp.where(mine, query_pair, 0)) for mine in masks]
        d_probs = [dot_cols(value_pair, jnp.where(mine, d_mixed_pair, 0)) for mine in masks]
        heads = (2 * pair, 2 * pair + 1)
        probs = [jnp.exp2(one * (LOG2E * scale) - stats_flat[h : h + 1, :]) for one, h in zip(scores, heads, strict=True)]
        d_scores = [
            (p * (d - inner_flat[h : h + 1, :])).astype(BF16) for p, d, h in zip(probs, d_probs, heads, strict=True)
        ]
        d_value = [dot(p.astype(BF16), d_mixed_pair) for p in probs]
        d_key = [dot(d, query_pair) for d in d_scores]
        d_query = [dot(key_flat[h * HEAD_DIM : (h + 1) * HEAD_DIM], d_scores[h]) for h in range(2)]
        d_query = jnp.transpose((jnp.concatenate(d_query, axis=0) * scale).astype(BF16))
        merge = lambda pieces: jnp.where(low_half, pieces[0], pieces[1])
        d_qkv_ref[0, :, at : at + LANES] = d_query
        d_qkv_ref[0, :, width + at : width + at + LANES] = jnp.where(inside, merge(d_key) * scale, 0.0).astype(BF16)
        d_qkv_ref[0, :, 2 * width + at : 2 * width + at + LANES] = jnp.where(inside, merge(d_value), 0.0).astype(BF16)


def feed_kernel(
    resid_ref, grad_ref, table_ref, first_bias_ref, w_first_ref, w_second_ref,
    out_ref, d_resid_ref, d_attn_ref, d_first_ref, d_second_ref, sums_ref, d_first_bias_ref,
    normed_ref, branch_ref, d_two_ref, active_ref, d_hidden_ref,
):
    step = pl.program_id(0)
    total_rows, width = resid_ref.shape
    block = w_first_ref.shape[1]
    tile = normed_ref.shape[0] // 4
    row = lambda index: table_ref[index : index + 1, :]

    @pl.when(step == 0)
    def _():
        unit_rows, _ = unit_parts(resid_ref[...])
        normed_ref[...] = (unit_rows * row(GAIN2) + row(SHIFT2)).astype(BF16)
        branch_ref[...] = jnp.zeros_like(branch_ref)
        d_two_ref[...] = jnp.zeros_like(d_two_ref)

    first_bias = first_bias_ref[0]
    bias_sum = jnp.zeros((1, block), F32)
    for part in range(total_rows // tile):
        here = slice(part * tile, (part + 1) * tile)
        hidden = dot(normed_ref[here, :], w_first_ref[...]) + first_bias
        bell = jnp.exp2(hidden * hidden * (-0.5 * LOG2E))
        near = 1.0 / (1.0 + (0.3275911 * 0.5**0.5) * jnp.abs(hidden))
        tail = 1.061405429 * near - 1.453152027
        tail = tail * near + 1.421413741
        tail = tail * near - 0.284496736
        tail = tail * near + 0.254829592
        tail = tail * near * bell * 0.5
        below = jnp.where(hidden >= 0.0, 1.0 - tail, tail)
        active = (hidden * below).astype(BF16)
        active_ref[here, :] = active
        branch_ref[here, :] += dot(active, w_second_ref[...])
        slope = below + hidden * bell * 0.3989422804014327
        d_hidden = dot_cols(grad_ref[here, :], w_second_ref[...]) * slope
        d_hidden = d_hidden.astype(BF16)
        d_hidden_ref[here, :] = d_hidden
        bias_sum += column_sum(d_hidden)
        d_two_ref[here, :] += dot_cols(d_hidden, w_first_ref[...])
    d_first_bias_ref[0] = bias_sum
    d_first_ref[...] = dot_rows(normed_ref[...], d_hidden_ref[...]).astype(BF16)
    d_second_ref[...] = dot_rows(active_ref[...], grad_ref[...]).astype(BF16)

    @pl.when(step == pl.num_programs(0) - 1)
    def _():
        resid = resid_ref[...]
        unit_rows, inverse = unit_parts(resid)
        out_ref[...] = (resid + branch_ref[...] + row(SECOND_BIAS)).astype(BF16)
        d_two = d_two_ref[...]
        sums_ref[0:1, :] = column_sum(d_two * unit_rows)
        sums_ref[1:2, :] = column_sum(d_two)
        sums_ref[2:3, :] = column_sum(grad_ref[...])
        d_resid = grad_ref[...].astype(F32) + norm_back(d_two, unit_rows, inverse, row(GAIN2))
        d_resid_ref[...] = d_resid
        d_attn = d_resid.astype(BF16)
        d_attn_ref[...] = d_attn
        sums_ref[3:4, :] = column_sum(d_attn)
        sums_ref[4:8, :] = jnp.zeros((4, width), F32)


def weight_grad_kernel(x_ref, table_ref, columns_ref, w_qkv_ref, d_qkv_ref, d_w_ref, sums_ref, norm_sums_ref, unit_ref):
    @pl.when(pl.program_id(0) == 0)
    def _():
        unit_rows, _ = unit_parts(x_ref[...].astype(F32))
        unit_ref[...] = jnp.transpose(unit_rows.astype(BF16))
        norm_sums_ref[...] = jnp.zeros_like(norm_sums_ref)

    d_qkv = d_qkv_ref[...]
    total = column_sum(d_qkv)
    unit_grad = dot(unit_ref[...], d_qkv)
    gain, shift = columns_ref[:, GAIN1 : GAIN1 + 1], columns_ref[:, SHIFT1 : SHIFT1 + 1]
    d_w_ref[...] = (unit_grad * gain + shift * total).astype(BF16)
    sums_ref[...] = jnp.broadcast_to(total, sums_ref.shape)
    weight = w_qkv_ref[...].astype(F32)
    norm_sums_ref[:, 0:1] += jnp.sum(unit_grad * weight, axis=1, keepdims=True)
    norm_sums_ref[:, 1:2] += jnp.sum(total * weight, axis=1, keepdims=True)


def input_grad_kernel(x_ref, table_ref, d_qkv_ref, w_qkv_ref, d_resid_ref, out_ref):
    d_one = dot_cols(d_qkv_ref[...], w_qkv_ref[...])
    unit_rows, inverse = unit_parts(x_ref[...].astype(F32))
    change = norm_back(d_one, unit_rows, inverse, table_ref[GAIN1 : GAIN1 + 1, :])
    out_ref[...] = (d_resid_ref[...] + change).astype(BF16)


def params():
    return pltpu.CompilerParams(vmem_limit_bytes=VMEM_BYTES)


def cost(*_):
    return pl.CostEstimate(flops=1, bytes_accessed=1, transcendentals=0)


def once(shape):
    zeros = (0,) * len(shape)
    return pl.BlockSpec(shape, lambda *_: zeros)


def attend(x, table, weights, length):
    count, seq, width = x.shape
    per_slot = lambda cols: pl.BlockSpec((1, seq, cols), lambda slot: (slot, 0, 0))
    rows = count * seq
    return pl.pallas_call(
        functools.partial(attend_kernel, length),
        grid=(count,),
        in_specs=[
            per_slot(width),
            once(table.shape),
            pl.BlockSpec((width, 3 * width), lambda slot: (0, 0)),
            pl.BlockSpec((width, width), lambda slot: (0, 3)),
        ],
        out_specs=[per_slot(3 * width), per_slot(width), per_slot(width), per_slot(LANES)],
        out_shape=[
            jax.ShapeDtypeStruct((count, seq, 3 * width), BF16),
            jax.ShapeDtypeStruct((count, seq, width), BF16),
            jax.ShapeDtypeStruct((count, seq, width), F32),
            jax.ShapeDtypeStruct((count, seq, LANES), F32),
        ],
        compiler_params=params(),
        cost_estimate=cost(12 * rows * width * width, rows * width * 14, rows * seq * 12),
    )(x, table, weights, weights)


def attend_back(d_attn, weights, qkv, mixed, stats, length, first, slots, written):
    count, seq, width = d_attn.shape
    per_slot = lambda cols: pl.BlockSpec((1, seq, cols), lambda slot: (first + slot, 0, 0))
    rows = slots * seq
    whole = [] if written is None else [written]
    kernel = functools.partial(attend_back_kernel, length)
    return pl.pallas_call(
        kernel if written is None else lambda *refs: kernel(*refs[:5], refs[6]),
        grid=(slots,),
        in_specs=[
            per_slot(width),
            pl.BlockSpec((width, width), lambda slot: (0, 3)),
            per_slot(3 * width),
            per_slot(width),
            per_slot(LANES),
        ]
        + [pl.BlockSpec(memory_space=pl.ANY)] * len(whole),
        out_specs=per_slot(3 * width),
        out_shape=jax.ShapeDtypeStruct((count, seq, 3 * width), BF16),
        input_output_aliases={5: 0} if whole else {},
        compiler_params=params(),
        cost_estimate=cost(10 * rows * width * width, rows * width * 16, rows * seq * 12),
    )(d_attn, weights, qkv, mixed, stats, *whole)


def feed(resid, grad, table, first_bias, weights):
    rows, width = resid.shape
    steps, _, block = first_bias.shape
    ff = steps * block
    column = lambda shift: pl.BlockSpec((width, block), lambda step: (0, 2 * step + shift))
    keep = lambda shape: pl.BlockSpec(shape, lambda step: (0, 0), pipeline_mode=pl.Buffered(1))
    return pl.pallas_call(
        feed_kernel,
        grid=(steps,),
        in_specs=[
            keep((rows, width)),
            keep((rows, width)),
            keep(table.shape),
            pl.BlockSpec((1, 1, block), lambda step: (step, 0, 0)),
            column(0),
            column(1),
        ],
        out_specs=[
            keep((rows, width)),
            keep((rows, width)),
            keep((rows, width)),
            pl.BlockSpec((width, block), lambda step: (0, step)),
            pl.BlockSpec((width, block), lambda step: (0, step)),
            keep((8, width)),
            pl.BlockSpec((1, 1, block), lambda step: (step, 0, 0)),
        ],
        out_shape=[
            jax.ShapeDtypeStruct((rows, width), BF16),
            jax.ShapeDtypeStruct((rows, width), F32),
            jax.ShapeDtypeStruct((rows, width), BF16),
            jax.ShapeDtypeStruct((width, ff + width), BF16),
            jax.ShapeDtypeStruct((width, ff), BF16),
            jax.ShapeDtypeStruct((8, width), F32),
            jax.ShapeDtypeStruct((steps, 1, block), F32),
        ],
        scratch_shapes=[
            pltpu.VMEM((rows, width), BF16),
            pltpu.VMEM((rows, width), F32),
            pltpu.VMEM((rows, width), F32),
            pltpu.VMEM((rows, block), BF16),
            pltpu.VMEM((rows, block), BF16),
        ],
        compiler_params=params(),
        cost_estimate=cost(12 * rows * width * ff, rows * width * 16 + 8 * width * ff, 2 * rows * ff),
    )(resid, grad, table, first_bias, weights, weights)


def weight_grad(x, table, columns, weights, d_qkv):
    rows, width = x.shape
    wide = d_qkv.shape[1]
    block = width
    keep = lambda shape: pl.BlockSpec(shape, lambda step: (0, 0), pipeline_mode=pl.Buffered(1))
    moving = lambda high: pl.BlockSpec((high, block), lambda step: (0, step))
    return pl.pallas_call(
        weight_grad_kernel,
        grid=(wide // block,),
        in_specs=[keep((rows, width)), keep(table.shape), keep(columns.shape), moving(width), moving(rows)],
        out_specs=[moving(width), moving(8), keep((width, LANES))],
        out_shape=[
            jax.ShapeDtypeStruct((width, wide + LANES), BF16),
            jax.ShapeDtypeStruct((8, wide), F32),
            jax.ShapeDtypeStruct((width, LANES), F32),
        ],
        scratch_shapes=[pltpu.VMEM((width, rows), BF16)],
        compiler_params=params(),
        cost_estimate=cost(2 * rows * width * wide, 2 * rows * (wide + width) + 4 * wide * width),
    )(x, table, columns, weights, d_qkv)


def input_grad(x, table, d_qkv, weights, d_resid):
    rows, width = x.shape
    wide = d_qkv.shape[1]
    tile = rows // 4
    part = lambda cols: pl.BlockSpec((tile, cols), lambda step: (step, 0))
    return pl.pallas_call(
        input_grad_kernel,
        grid=(rows // tile,),
        in_specs=[
            part(width),
            once(table.shape),
            part(wide),
            pl.BlockSpec((width, wide), lambda step: (0, 0)),
            part(width),
        ],
        out_specs=part(width),
        out_shape=jax.ShapeDtypeStruct((rows, width), BF16),
        compiler_params=params(),
        cost_estimate=cost(2 * rows * width * wide, rows * (2 * wide + 8 * width)),
    )(x, table, d_qkv, weights, d_resid)


def gather(value):
    return lax.all_gather(value, "fsdp", axis=0, tiled=True)


def scatter(value):
    return lax.psum_scatter(value, "fsdp", scatter_dimension=0, tiled=True)


def swap(value, bit, devices):
    return lax.ppermute(value, "fsdp", [(i, i ^ bit) for i in range(devices)])


def my_bit(bit):
    return (lax.axis_index("fsdp") // bit) % 2


def bit_orders(devices):
    bits = [1 << k for k in range(1, devices.bit_length() - 1)]
    near, far = bits[:3], bits[3:]
    return [near[k:] + near[:k] + far for k in range(3)]


def pair_up(mine, other, axis, bit):
    shape = mine.shape[:axis] + (2,) + mine.shape[axis:]
    is_mine = lax.broadcasted_iota(jnp.int32, shape, axis) == my_bit(bit)
    return jnp.where(is_mine, jnp.expand_dims(mine, axis), jnp.expand_dims(other, axis))


def tie(first, second):
    count = len(first)
    both = lax.optimization_barrier((*first, *second))
    return list(both[:count]), list(both[count:])


def pair_gather(shard, devices, raw, meanwhile):
    own = shard.shape[0]
    third = own // 3
    orders = bit_orders(devices)
    near = len({order[0] for order in orders})
    held = []
    for bit in reversed(orders[0][near:]):
        shard = pair_up(shard, swap(shard, bit, devices), len(held), bit)
        held.append(bit)
    parts = [shard[..., k * third : (k + 1) * third, :] for k in range(3)]
    held = [list(held) for _ in range(3)]
    for level in reversed(range(near)):
        if level == 0:
            parts, raw = tie(parts, raw)
        others = [swap(part, order[level], devices) for part, order in zip(parts, orders, strict=True)]
        if level == 0:
            others, extra = tie(others, meanwhile(*raw))
        for k, order in enumerate(orders):
            axis = sum(one > order[level] for one in held[k])
            held[k].append(order[level])
            parts[k] = pair_up(parts[k], others[k], axis, order[level])
    mine = jnp.concatenate([part.reshape(devices // 2, third, -1) for part in parts], axis=1)
    whole = pair_up(mine, swap(mine, 1, devices), 1, 1)
    return whole.reshape(devices * own, -1), extra


def add(left, right):
    return left.astype(F32) + right.astype(F32)


def fold_kernel(spans, widths, first, joined, bits_ref, *refs):
    split = 2 if first else len(refs) - (2 if joined else 2 * len(widths))
    ins, outs = refs[:split], refs[split:]
    at = 0
    for k, (span, width) in enumerate(zip(spans, widths, strict=True)):
        cut = slice(at, at + width)
        for side in range(2):
            out_ref = outs[side] if joined else outs[2 * k + side]
            which = 1 - bits_ref[k] if side == 0 else bits_ref[k]
            for j in range(out_ref.shape[0]):
                i = j // span * (2 * span) + which * span + j % span
                if first:
                    kept, came = ins[0][i, 0, :, cut], ins[1][i, :, cut]
                else:
                    kept, came = ins[k][i], ins[split // 2 + k][i]
                if joined:
                    out_ref[j, :, cut] = add(kept, came).astype(BF16)
                else:
                    out_ref[j] = add(kept, came).astype(BF16)
        at += width


class PairScatter:
    def __init__(self, value, devices):
        self.devices = devices
        self.orders = bit_orders(devices)
        self.left = [sorted(order, reverse=True) for order in self.orders]
        self.level = 0
        tiles = value.shape[1] // LANES
        self.widths = [(tiles + 2 - k) // 3 * LANES for k in range(3)]
        self.keep = [value.reshape(devices // 2, 2, -1, value.shape[1])]
        self.sends = [lax.dynamic_index_in_dim(self.keep[0], 1 - my_bit(1), 1, keepdims=False)]
        self.bits = [1]

    def swap(self):
        self.coming = [swap(send, bit, self.devices) for send, bit in zip(self.sends, self.bits, strict=True)]

    def beside(self, inputs, compute):
        self.sends, inputs = tie(self.sends, inputs)
        self.swap()
        self.coming, results = tie(self.coming, compute(*inputs))
        return results

    def fold(self):
        first = self.level == 0
        self.bits = [order[self.level] for order in self.orders]
        places = [left.index(bit) for left, bit in zip(self.left, self.bits, strict=True)]
        spans = [1 << (len(left) - 1 - place) for left, place in zip(self.left, places, strict=True)]
        for left, place in zip(self.left, places, strict=True):
            left.pop(place)
        joined = len(set(self.bits)) == 1
        count, own = self.coming[0].shape[:2]
        chosen = jnp.stack([my_bit(bit) for bit in (*self.bits, 1)]).astype(jnp.int32)
        whole = lambda shape: pl.BlockSpec(shape, lambda step, bits: (0,) * len(shape))
        if first:
            core = len(self.bits)
            kept_specs = [pl.BlockSpec((count, 1, *self.keep[0].shape[2:]), lambda step, bits: (0, bits[core], 0, 0))]
        else:
            kept_specs = [whole(one.shape) for one in self.keep]
        widths = [sum(self.widths)] if joined else self.widths
        out_shapes = [(count // 2, own, width) for width in widths for _ in range(2)]
        folded = pl.pallas_call(
            functools.partial(fold_kernel, spans, self.widths, first, joined),
            grid_spec=pltpu.PrefetchScalarGridSpec(
                num_scalar_prefetch=1,
                grid=(1,),
                in_specs=kept_specs + [whole(one.shape) for one in self.coming],
                out_specs=[whole(shape) for shape in out_shapes],
            ),
            out_shape=[jax.ShapeDtypeStruct(shape, BF16) for shape in out_shapes],
            compiler_params=params(),
            cost_estimate=cost(),
        )(chosen, *self.keep, *self.coming)
        self.sends, self.keep = list(folded[::2]), list(folded[1::2])
        self.level += 1
        if joined:
            self.widths, self.bits = widths, self.bits[:1]
            self.orders, self.left = self.orders[:1], self.left[:1]

    def finish(self):
        while self.level < len(self.orders[0]):
            self.fold()
            self.swap()

    def result(self):
        return jnp.concatenate([add(one, two)[0] for one, two in zip(self.keep, self.coming, strict=True)], axis=-1)


def on_device(
    images,
    images_of,
    cotangent,
    ln1_gain,
    ln1_shift,
    w_qkv,
    query_bias,
    value_bias,
    w_out,
    out_bias,
    ln2_gain,
    ln2_shift,
    w_first,
    first_bias,
    w_second,
    second_bias,
):
    devices = lax.axis_size("fsdp")
    count, length, width = images.shape
    own = w_qkv.shape[0]
    wide = w_qkv.shape[1]
    ff = w_first.shape[1]
    chunks = ff // width
    seq = -(-length // ROW_TILE) * ROW_TILE
    rows = count * seq
    slot_index = jnp.arange(count, dtype=jnp.int32)
    slot_live = (slot_index % 2 < jnp.repeat(images_of, 2)).astype(BF16)[:, None, None]

    small = jnp.stack(
        [ln1_gain, ln1_shift, query_bias, value_bias, out_bias, ln2_gain, ln2_shift, second_bias], axis=1
    )
    small = jnp.concatenate([small, first_bias.reshape(own, chunks)], axis=1)
    small = jnp.pad(small, ((0, 0), (0, LANES - small.shape[1])))
    first_parts = w_first.reshape(own, width, chunks).transpose(0, 2, 1)
    feed_shard = jnp.stack([first_parts, w_second.reshape(own, chunks, width)], axis=2)
    pad = ((0, 0), (0, seq - length), (0, 0))
    attn_weights, (x, grad) = pair_gather(
        jnp.concatenate([w_qkv, w_out, small], axis=1),
        devices,
        [images, cotangent],
        lambda x, grad: [jnp.pad(x, pad), jnp.pad(grad * slot_live, pad)],
    )
    grad = grad.reshape(rows, width)
    feed_weights = gather(feed_shard.reshape(own, 2 * ff))
    columns = attn_weights[:, wide + width :].astype(F32)
    table = columns[:, :16].T
    bias_rows = table[8 : 8 + chunks].reshape(chunks, 1, width)

    qkv, mixed, resid, stats = attend(x, table, attn_weights, length)
    out, d_resid, d_attn, d_feed, d_second, feed_sums, d_first_bias = feed(
        resid.reshape(rows, width), grad, table, bias_rows, feed_weights
    )
    d_second = scatter(d_second)
    d_w_out = dot_rows(mixed.reshape(rows, width), d_attn).astype(BF16)
    feed_grads = PairScatter(lax.dynamic_update_slice(d_feed, d_w_out, (0, ff)), devices)
    back = lambda first, slots: (
        lambda d_attn, *written: [
            attend_back(d_attn, attn_weights, qkv, mixed, stats, length, first, slots, *(written or [None]))
        ]
    )
    d_attn = d_attn.reshape(count, seq, width)
    few = max(count // 4, 1)
    (d_qkv,) = feed_grads.beside([d_attn], back(0, few))
    feed_grads.keep, (d_qkv,) = tie(feed_grads.keep, [d_qkv])
    feed_grads.fold()
    (d_qkv,) = feed_grads.beside([d_attn, d_qkv], back(few, count - few))
    d_qkv = d_qkv.reshape(rows, wide)
    x_rows = x.reshape(rows, width)
    feed_grads.fold()
    d_w_qkv, qkv_sums, norm_sums = feed_grads.beside(
        [d_qkv], lambda d_qkv: weight_grad(x_rows, table, columns, attn_weights, d_qkv)
    )
    feed_grads.fold()
    feed_grads.sends, (d_w_qkv, qkv_sums, norm_sums) = tie(feed_grads.sends, [d_w_qkv, qkv_sums, norm_sums])
    feed_grads.swap()
    ends = jnp.concatenate(
        [
            norm_sums[:, :2],
            qkv_sums[0, :width][:, None],
            qkv_sums[0, 2 * width :][:, None],
            feed_sums[:4].T,
            d_first_bias.reshape(chunks, width).T,
        ],
        axis=1,
    )
    ends = jnp.pad(ends, ((0, 0), (0, LANES - ends.shape[1]))).astype(BF16)
    qkv_grads = PairScatter(lax.dynamic_update_slice(d_w_qkv, ends, (0, wide)), devices)
    qkv_grads.sends, feed_grads.keep = tie(qkv_grads.sends, feed_grads.keep)
    qkv_grads.swap()
    feed_grads.fold()
    feed_grads.sends, qkv_grads.keep = tie(feed_grads.sends, qkv_grads.keep)
    feed_grads.swap()
    qkv_grads.fold()
    (d_x,) = qkv_grads.beside(
        [d_qkv, d_resid], lambda d_qkv, d_resid: [input_grad(x_rows, table, d_qkv, attn_weights, d_resid)]
    )
    feed_grads.coming, qkv_grads.keep = tie(feed_grads.coming, qkv_grads.keep)
    qkv_grads.fold()
    qkv_grads.sends, (d_x, out) = tie(qkv_grads.sends, [d_x, out])
    qkv_grads.swap()
    output = out.reshape(count, seq, width)[:, :length] * slot_live
    d_x = d_x.reshape(count, seq, width)[:, :length]
    qkv_grads.coming, (output, d_x) = tie(qkv_grads.coming, [output, d_x])
    qkv_grads.fold()
    qkv_grads.sends, feed_grads.keep = tie(qkv_grads.sends, feed_grads.keep)
    qkv_grads.swap()
    feed_grads.finish()
    d_feed = feed_grads.result()
    d_second, (d_feed,) = tie([d_second], [d_feed])
    d_w_out = d_feed[:, ff:]
    d_w_first = d_feed[:, :ff].reshape(own, chunks, width).transpose(0, 2, 1).reshape(own, ff)
    d_w_second = d_second[0].astype(F32).reshape(own * chunks, width)
    qkv_grads.coming, (d_w_out, d_w_first, d_w_second) = tie(qkv_grads.coming, [d_w_out, d_w_first, d_w_second])
    qkv_grads.finish()
    d_qkv_all = qkv_grads.result()

    d_w_qkv = d_qkv_all[:, :wide]
    ends = d_qkv_all[:, wide:]
    return (
        output,
        d_x,
        ends[:, 0],
        ends[:, 1],
        d_w_qkv,
        ends[:, 2],
        ends[:, 3],
        d_w_out,
        ends[:, 7],
        ends[:, 4],
        ends[:, 5],
        d_w_first,
        ends[:, 8 : 8 + chunks].reshape(own * chunks),
        d_w_second,
        ends[:, 6],
    )


def solution(mesh):
    flat, rows = P("fsdp"), P("fsdp", None)
    slots = P("fsdp", None, None)
    placed = (slots, flat, slots, flat, flat, rows, flat, flat, rows, flat, flat, flat, rows, flat, rows, flat)
    outs = (slots, slots, flat, flat, rows, flat, flat, rows, flat, flat, flat, rows, flat, rows, flat)
    return jax.shard_map(on_device, mesh=mesh, in_specs=placed, out_specs=outs, check_vma=False)
```
